32 devices in a mesh: sensor: 8 (over z, y), param: 4 (over x, core).
Axes of the slice: x: 2, y: 2, z: 4, core: 2. Of those that a mesh axis runs over, the one named last changes fastest.
Arguments:
- parameter_field: float32 [8, 192, 420], P(None, ('param', 'sensor')), may hold values from -6 to 6
- operator_blocks: float32 [2, 421, 8, 4, 384], P(None, None, 'sensor', 'param'), may hold values from -0.625 to 0.625
- noise_weights: float32 [64, 420], P('sensor'), may hold values from 0.25 to 4
Outputs:
- hessian_action: float32 [8, 192, 420], P(None, ('param', 'sensor'))
The draws below stay inside these ranges and needn't reach their ends.
All inputs are finite; a program needn't handle non-finite values.
Results may differ from the reference program's by a relative error of at most 0.000071.
Values sent between devices are 32-bit elements; how exact they have to be, the bound alone decides.
A program may use at most 64 MiB of HBM per device.

```python
import math
import jax
import jax.numpy as jnp
from jax import lax

NT = 420
NF = 421
SENS_DEV = 8
PAR_DEV = 48
NVEC = 8
SENSORS = 64
PARAMS = 192
N_SENSOR = 8
N_PARAM = 4


def with_spikes(values, own_key, source, target, parts, factor):
    def block_of(position):
        return (jnp.arange(values.shape[position]) // (values.shape[position] // parts)).reshape((-1,) + (1,) * (values.ndim - 1 - position))

    first = jax.random.permutation(own_key, parts)[block_of(target)]
    second = (block_of(target) + parts // 2) % parts
    return jnp.where((block_of(source) == first) | (block_of(source) == second), factor * values, values)


def levels(key, shape, shards, least, high):
    def one(position, parts):
        steps = jax.random.uniform(jax.random.fold_in(jax.random.fold_in(key, 6), position), (parts,), jnp.float32, least / len(shards), high / len(shards))
        return jnp.repeat(jnp.exp(steps), shape[position] // parts).reshape((-1,) + (1,) * (len(shape) - position - 1))

    factor_of = one(*shards[0])
    for cut in shards[1:]:
        factor_of = factor_of * one(*cut)
    return factor_of


def gaussian(own_key, shape, deviation, most, cuts=(), held_as=jnp.bfloat16):
    level = levels(own_key, shape, cuts, -0.22, 0.18) if cuts else 1.0
    entries = jax.random.normal(own_key, shape, jnp.float32) * deviation * level
    return jnp.minimum(jnp.maximum(entries, -most), most).astype(held_as)


def heavy_noise(rng, dims, deviation, reach, pieces, heavy, kind=jnp.bfloat16):
    drawn = deviation * jax.random.normal(rng, dims, jnp.float32)
    if pieces:
        drawn = drawn * levels(rng, dims, pieces, -0.22, 0.18)
    return jnp.clip(with_spikes(drawn, jax.random.fold_in(rng, 3), *heavy), -reach, reach).astype(kind)


def setup_inputs(seed: int = 0) -> dict:
    arg_keys = jax.random.split(jax.random.key(seed), 4)
    parameter_field = gaussian(arg_keys[0], (NVEC, PARAMS, NT), 1.0, 6.0, ((1, 32),), jnp.float32)
    operator_blocks = heavy_noise(arg_keys[1], (2, NF, N_SENSOR, N_PARAM, PAR_DEV * SENS_DEV), PARAMS ** -0.5, 0.625, ((2, 8), (3, 4)), (2, 4, 8, 2.0), jnp.float32)
    noise_weights = jnp.clip(jnp.exp(math.log(4.0) - 2.7725887 * jax.random.uniform(arg_keys[2], (SENSORS, NT), jnp.float32) ** levels(arg_keys[2], (SENSORS, NT), ((0, 8),), -0.2, 0.2)), 0.25, 4.0)
    return {"parameter_field": parameter_field, "operator_blocks": operator_blocks, "noise_weights": noise_weights}


highest = lax.Precision.HIGHEST


def product(form, left, right):
    return jnp.einsum(form, left, right, precision=highest)


def reference(parameter_field, operator_blocks, noise_weights):
    length = 2 * NT
    tiled = operator_blocks.reshape(2, NF, N_SENSOR, N_PARAM, PAR_DEV, SENS_DEV)
    whole_blocks = jnp.transpose(tiled, (0, 1, 2, 5, 3, 4)).reshape(2, NF, SENSORS, PARAMS)
    real_blocks = whole_blocks[0]
    imag_blocks = whole_blocks[1]
    spectrum = jnp.fft.rfft(parameter_field, n=length, axis=-1)
    field_real = jnp.transpose(jnp.real(spectrum), (2, 0, 1))
    field_imag = jnp.transpose(jnp.imag(spectrum), (2, 0, 1))
    pred_real = product("ksp,kvp->kvs", real_blocks, field_real) - product("ksp,kvp->kvs", imag_blocks, field_imag)
    pred_imag = product("ksp,kvp->kvs", real_blocks, field_imag) + product("ksp,kvp->kvs", imag_blocks, field_real)
    predicted = lax.complex(jnp.transpose(pred_real, (1, 2, 0)), jnp.transpose(pred_imag, (1, 2, 0)))
    data = jnp.fft.irfft(predicted, n=length, axis=-1)[..., :NT]
    weighted = data * noise_weights[None, :, :]
    weighted_spectrum = jnp.fft.rfft(weighted, n=length, axis=-1)
    data_real = jnp.transpose(jnp.real(weighted_spectrum), (2, 0, 1))
    data_imag = jnp.transpose(jnp.imag(weighted_spectrum), (2, 0, 1))
    adj_real = product("ksp,kvs->kvp", real_blocks, data_real) + product("ksp,kvs->kvp", imag_blocks, data_imag)
    adj_imag = product("ksp,kvs->kvp", real_blocks, data_imag) - product("ksp,kvs->kvp", imag_blocks, data_real)
    adjoint_spectrum = lax.complex(jnp.transpose(adj_real, (1, 2, 0)), jnp.transpose(adj_imag, (1, 2, 0)))
    return jnp.fft.irfft(adjoint_spectrum, n=length, axis=-1)[..., :NT]
```

```python
import functools
import math

import jax
import jax.numpy as jnp
import ml_dtypes
import numpy as np
from jax import lax
from jax.experimental import pallas as pl
from jax.experimental.pallas import tpu as pltpu
from jax.sharding import PartitionSpec as P

LANES = 128
f32 = jnp.float32
bf16 = jnp.bfloat16


def round_up(value, step):
    return -(-value // step) * step


def split_table(table):
    high = table.astype(ml_dtypes.bfloat16)
    low = (table - high.astype(np.float64)).astype(ml_dtypes.bfloat16)
    return np.stack([high, low])


def tables(time_steps):
    length = 2 * time_steps
    freq_count = time_steps + 1
    time_pad = round_up(time_steps, LANES)
    freq_pad = round_up(freq_count, LANES)
    angles = (np.arange(time_steps)[:, None] * np.arange(freq_count)[None, :] % length) * (
        2.0 * math.pi / length
    )
    factor = np.full(freq_count, 2.0)
    factor[0] = factor[-1] = 1.0
    factor /= length
    forward = np.zeros((time_pad, 2 * freq_pad))
    forward[:time_steps, :freq_count] = np.cos(angles)
    forward[:time_steps, freq_pad : freq_pad + freq_count] = -np.sin(angles)
    inverse = np.zeros((2 * freq_pad, time_pad))
    inverse[:freq_count, :time_steps] = factor[:, None] * np.cos(angles).T
    inverse[freq_pad : freq_pad + freq_count, :time_steps] = -factor[:, None] * np.sin(angles).T
    return split_table(forward), split_table(inverse)


def product(left, table_ref, depth):
    high = left.astype(bf16)
    low = (left - high.astype(f32)).astype(bf16)
    table_high = table_ref[0, :depth]
    table_low = table_ref[1, :depth]

    def dot(a, b):
        return jnp.dot(a, b, preferred_element_type=f32)

    return dot(low, table_high) + dot(high, table_low) + dot(high, table_high)


def kernel(
    sizes,
    x_ref,
    blocks_ref,
    weights_ref,
    fwd_hbm,
    inv_hbm,
    out_ref,
    raw,
    ft,
    fwd,
    inv,
    xg,
    xs,
    ps,
    part,
    part_in,
    wexp,
    wdat,
    gs,
    gout,
    y_in,
    z_out,
    z_in,
    local_sem,
    gz_s,
    gz_r,
    gy_s,
    gy_r,
    ps_s,
    ps_r,
    pg_s,
    pg_r,
    ry_s,
    ry_r,
    rz_s,
    rz_r,
):
    vecs, own_pars, steps, sens, pars, n_sensor, n_param, fast = sizes
    slow = n_sensor // fast
    freqs = steps + 1
    freq_pad = round_up(freqs, LANES)
    tiles = freq_pad // LANES
    group_pars = fast * own_pars
    chunk = own_pars * vecs
    group_rows = group_pars * vecs
    rows = sens * vecs
    share = rows // n_param
    unroll = 4 if group_pars % 4 == 0 else 1

    me = lax.axis_index("sensor")
    mp = lax.axis_index("param")
    mz = me // fast
    my = me % fast
    y_peer = mz * fast + (1 - my)

    def z_at(distance):
        return lax.rem(mz + distance, slow)

    def z_back(distance):
        return lax.rem(mz + slow - distance, slow)

    def p_at(distance):
        return lax.rem(mp + distance, n_param)

    def p_back(distance):
        return lax.rem(mp + n_param - distance, n_param)

    def to_sensor(target, src, dst, send, recv):
        return pltpu.make_async_remote_copy(
            src_ref=src, dst_ref=dst, send_sem=send, recv_sem=recv,
            device_id=(target, mp), device_id_type=pl.DeviceIdType.MESH,
        )

    def to_param(target, src, dst, send, recv):
        return pltpu.make_async_remote_copy(
            src_ref=src, dst_ref=dst, send_sem=send, recv_sem=recv,
            device_id=(me, target), device_id_type=pl.DeviceIdType.MESH,
        )

    barrier = pltpu.get_barrier_semaphore()

    def greet(device):
        pl.semaphore_signal(barrier, inc=1, device_id=device, device_id_type=pl.DeviceIdType.MESH)

    greet((y_peer, mp))
    for d in range(1, slow):
        greet((z_at(d) * fast + my, mp))
    for j in range(1, n_param):
        greet((me, p_at(j)))

    blocks_rows = blocks_ref.shape[0]
    load_blocks = pltpu.make_async_copy(
        blocks_ref.at[:, 0], raw.at[pl.ds(0, blocks_rows)], local_sem.at[0]
    )
    load_blocks.start()
    load_fwd = pltpu.make_async_copy(fwd_hbm, fwd, local_sem.at[1])
    load_fwd.start()
    load_inv = pltpu.make_async_copy(inv_hbm, inv, local_sem.at[2])
    load_inv.start()
    pl.semaphore_wait(barrier, 1 + (slow - 1) + (n_param - 1))

    own_y = to_sensor(y_peer, x_ref, xg.at[me], gy_s.at[0], gy_r.at[0])
    own_y.start()
    own_z = {}
    for d in range(1, slow):
        own_z[d] = to_sensor(z_at(d) * fast + my, x_ref, xg.at[me], gz_s.at[d], gz_r.at[d])
        own_z[d].start()

    xg[me] = x_ref[...]
    spread = jnp.concatenate(
        [jnp.broadcast_to(weights_ref[r : r + 1], (vecs, steps)) for r in range(sens)], axis=0
    )
    for i in range(n_param):
        wexp[i] = spread[i * share : (i + 1) * share]

    def turn(part_index, tile):
        width_tiles = (pars * sens) // LANES
        first = pl.multiple_of(tile * LANES, LANES)
        inside = first + lax.broadcasted_iota(jnp.int32, (LANES, LANES), 1) < freqs
        for w in range(width_tiles):
            start = (part_index * freqs + first) * width_tiles + w
            block = raw[pl.ds(start, LANES, stride=width_tiles), :]
            turned = jnp.where(inside, block.T, 0.0)
            per = LANES // sens
            ft[part_index, w * per : (w + 1) * per, :, pl.ds(first, LANES)] = turned.reshape(
                per, sens, LANES
            )

    forwards = {}

    def forward_chunk(d):
        own_z[d].wait_recv()
        source = z_back(d) * fast + my
        forwards[d] = to_sensor(y_peer, xg.at[source], xg.at[source], gy_s.at[d], gy_r.at[d])
        forwards[d].start()

    load_blocks.wait()

    def turn_tile(tile, carry):
        turn(0, tile)
        turn(1, tile)
        return carry

    ready = [d for d in range(1, slow)]
    half = max(tiles // 2, 1)
    lax.fori_loop(0, half, turn_tile, 0)
    for d in ready[:1]:
        forward_chunk(d)
    lax.fori_loop(half, tiles, turn_tile, 0)
    for d in ready[1:]:
        forward_chunk(d)
    load_fwd.wait()

    def lanes_of(tile, c):
        return pl.ds(pl.multiple_of(tile * LANES + c * freq_pad, LANES), LANES)

    def forward_group(zz, initial):
        field = xg[pl.ds(zz * fast, fast)].reshape(group_rows, steps)
        xs[...] = product(field, fwd, steps).reshape(group_pars, vecs, 2 * freq_pad)
        base = zz * group_pars

        def tile_step(tile, carry):
            re, im = lanes_of(tile, 0), lanes_of(tile, 1)
            if initial:
                acc = tuple(jnp.zeros((vecs, LANES), f32) for _ in range(2 * sens))
            else:
                acc = tuple(ps[r, :, re] for r in range(sens)) + tuple(
                    ps[r, :, im] for r in range(sens)
                )

            def par_step(step, acc):
                acc = list(acc)
                for u in range(unroll):
                    q = step * unroll + u
                    xr, xi = xs[q, :, re], xs[q, :, im]
                    for r in range(sens):
                        fr = ft[0, base + q, r : r + 1, re]
                        fi = ft[1, base + q, r : r + 1, re]
                        acc[r] = acc[r] + fr * xr - fi * xi
                        acc[sens + r] = acc[sens + r] + fr * xi + fi * xr
                return tuple(acc)

            acc = lax.fori_loop(0, group_pars // unroll, par_step, acc)
            for r in range(sens):
                ps[r, :, re] = acc[r]
                ps[r, :, im] = acc[sens + r]
            return carry

        lax.fori_loop(0, tiles, tile_step, 0)

    for d in range(slow):
        if d == 0:
            own_y.wait_recv()
        else:
            forwards[d].wait_recv()
        forward_group(z_back(d), d == 0)

    load_inv.wait()
    series = product(ps[...].reshape(rows, 2 * freq_pad), inv, 2 * freq_pad)
    for i in range(n_param):
        part[i] = series[i * share : (i + 1) * share, :steps]
    sums = {}
    for j in range(1, n_param):
        sums[j] = to_param(p_at(j), part.at[p_at(j)], part_in.at[j], ps_s.at[j], ps_r.at[j])
        sums[j].start()
    total = part[mp]
    for j in range(1, n_param):
        sums[j].wait_recv()
        total = total + part_in[j]
    wdat[mp] = total * wexp[mp]
    spreads = {}
    for j in range(1, n_param):
        spreads[j] = to_param(p_at(j), wdat.at[mp], wdat.at[mp], pg_s.at[j], pg_r.at[j])
        spreads[j].start()
    for j in range(1, n_param):
        spreads[j].wait_recv()
    weighted = jnp.concatenate([wdat[i] for i in range(n_param)], axis=0)
    ps[...] = product(weighted, fwd, steps).reshape(sens, vecs, 2 * freq_pad)

    def adjoint_group(zz, slot):
        base = zz * group_pars

        def tile_step(tile, carry):
            re, im = lanes_of(tile, 0), lanes_of(tile, 1)
            wr = [ps[r, :, re] for r in range(sens)]
            wi = [ps[r, :, im] for r in range(sens)]

            def par_step(step, carry):
                for u in range(unroll):
                    q = step * unroll + u
                    gr = jnp.zeros((vecs, LANES), f32)
                    gi = jnp.zeros((vecs, LANES), f32)
                    for r in range(sens):
                        fr = ft[0, base + q, r : r + 1, re]
                        fi = ft[1, base + q, r : r + 1, re]
                        gr = gr + fr * wr[r] + fi * wi[r]
                        gi = gi + fr * wi[r] - fi * wr[r]
                    gs[q, :, re] = gr
                    gs[q, :, im] = gi
                return carry

            return lax.fori_loop(0, group_pars // unroll, par_step, carry)

        lax.fori_loop(0, tiles, tile_step, 0)
        result = product(gs[...].reshape(group_rows, 2 * freq_pad), inv, 2 * freq_pad)
        for y in range(fast):
            gout[slot, y] = result[y * chunk : (y + 1) * chunk, :steps]

    y_sends, z_sends = {}, {}

    def pass_on(d):
        y_sends[d].wait_recv()
        z_out[d] = gout[d, my] + y_in[d]
        z_sends[d] = to_sensor(z_at(d) * fast + my, z_out.at[d], z_in.at[d], rz_s.at[d], rz_r.at[d])
        z_sends[d].start()

    order = list(range(slow - 1, -1, -1))
    for place, d in enumerate(order):
        adjoint_group(z_at(d), d)
        y_sends[d] = to_sensor(y_peer, gout.at[d, 1 - my], y_in.at[d], ry_s.at[d], ry_r.at[d])
        y_sends[d].start()
        if place:
            pass_on(order[place - 1])
    y_sends[0].wait_recv()
    answer = gout[0, my] + y_in[0]
    for d in order[:-1]:
        z_sends[d].wait_recv()
        answer = answer + z_in[d]
    out_ref[...] = answer

    own_y.wait_send()
    for d in range(1, slow):
        own_z[d].wait_send()
        forwards[d].wait_send()
        z_sends[d].wait_send()
    for d in range(slow):
        y_sends[d].wait_send()
    for j in range(1, n_param):
        sums[j].wait_send()
        spreads[j].wait_send()


def shards(n_sensor, n_param, parameter_field, operator_blocks, noise_weights):
    vecs, own_pars, steps = parameter_field.shape
    sens = noise_weights.shape[0]
    freqs = steps + 1
    flat_width = operator_blocks.shape[4]
    pars = flat_width // sens
    fast = 2
    slow = n_sensor // fast
    chunk = own_pars * vecs
    group_pars = fast * own_pars
    share = sens * vecs // n_param
    freq_pad = round_up(freqs, LANES)
    width_tiles = flat_width // LANES
    forward_table, inverse_table = tables(steps)
    field = jnp.transpose(parameter_field, (1, 0, 2)).reshape(chunk, steps)
    blocks = operator_blocks.reshape(2 * freqs * width_tiles, 1, LANES)
    sizes = (vecs, own_pars, steps, sens, pars, n_sensor, n_param, fast)
    raw_rows = round_up((freqs + freq_pad) * width_tiles, 8)
    vmem = pl.BlockSpec(memory_space=pltpu.VMEM)
    anywhere = pl.BlockSpec(memory_space=pl.ANY)
    dma = pltpu.SemaphoreType.DMA
    result = pl.pallas_call(
        functools.partial(kernel, sizes),
        out_shape=jax.ShapeDtypeStruct((chunk, steps), f32),
        in_specs=[vmem, anywhere, vmem, anywhere, anywhere],
        out_specs=vmem,
        scratch_shapes=[
            pltpu.VMEM((raw_rows, LANES), f32),
            pltpu.VMEM((2, pars, sens, freq_pad), f32),
            pltpu.VMEM(forward_table.shape, bf16),
            pltpu.VMEM(inverse_table.shape, bf16),
            pltpu.VMEM((n_sensor, chunk, steps), f32),
            pltpu.VMEM((group_pars, vecs, 2 * freq_pad), f32),
            pltpu.VMEM((sens, vecs, 2 * freq_pad), f32),
            pltpu.VMEM((n_param, share, steps), f32),
            pltpu.VMEM((n_param, share, steps), f32),
            pltpu.VMEM((n_param, share, steps), f32),
            pltpu.VMEM((n_param, share, steps), f32),
            pltpu.VMEM((group_pars, vecs, 2 * freq_pad), f32),
            pltpu.VMEM((slow, fast, chunk, steps), f32),
            pltpu.VMEM((slow, chunk, steps), f32),
            pltpu.VMEM((slow, chunk, steps), f32),
            pltpu.VMEM((slow, chunk, steps), f32),
            dma((3,)),
            dma((slow,)),
            dma((slow,)),
            dma((slow,)),
            dma((slow,)),
            dma((n_param,)),
            dma((n_param,)),
            dma((n_param,)),
            dma((n_param,)),
            dma((slow,)),
            dma((slow,)),
            dma((slow,)),
            dma((slow,)),
        ],
        compiler_params=pltpu.CompilerParams(
            collective_id=0, has_side_effects=True, vmem_limit_bytes=40 * 1024 * 1024
        ),
    )(field, blocks, noise_weights, jnp.asarray(forward_table), jnp.asarray(inverse_table))
    return jnp.transpose(result.reshape(own_pars, vecs, steps), (1, 0, 2))


def solution(mesh):
    in_specs = (
        P(None, ("param", "sensor"), None),
        P(None, None, "sensor", "param", None),
        P("sensor", None),
    )
    out_specs = P(None, ("param", "sensor"), None)
    run = functools.partial(shards, mesh.shape["sensor"], mesh.shape["param"])
    return jax.shard_map(run, mesh=mesh, in_specs=in_specs, out_specs=out_specs, check_vma=False)
```

```python
import functools
import math

import jax
import jax.numpy as jnp
import ml_dtypes
import numpy as np
from jax import lax
from jax.experimental import pallas as pl
from jax.experimental.pallas import tpu as pltpu
from jax.sharding import PartitionSpec as P

LANES = 128
f32 = jnp.float32
bf16 = jnp.bfloat16


def round_up(value, step):
    return -(-value // step) * step


def split_table(table):
    high = table.astype(ml_dtypes.bfloat16)
    low = (table - high.astype(np.float64)).astype(ml_dtypes.bfloat16)
    return np.stack([high, low])


def tables(time_steps):
    length = 2 * time_steps
    freq_count = time_steps + 1
    time_pad = round_up(time_steps, LANES)
    freq_pad = round_up(freq_count, LANES)
    angles = (np.arange(time_steps)[:, None] * np.arange(freq_count)[None, :] % length) * (
        2.0 * math.pi / length
    )
    factor = np.full(freq_count, 2.0)
    factor[0] = factor[-1] = 1.0
    factor /= length
    forward = np.zeros((time_pad, 2 * freq_pad))
    forward[:time_steps, :freq_count] = np.cos(angles)
    forward[:time_steps, freq_pad : freq_pad + freq_count] = -np.sin(angles)
    inverse = np.zeros((2 * freq_pad, time_pad))
    inverse[:freq_count, :time_steps] = factor[:, None] * np.cos(angles).T
    inverse[freq_pad : freq_pad + freq_count, :time_steps] = -factor[:, None] * np.sin(angles).T
    return split_table(forward), split_table(inverse)


def product(left, table_ref, depth):
    high = left.astype(bf16)
    low = (left - high.astype(f32)).astype(bf16)
    table_high = table_ref[0, :depth]
    table_low = table_ref[1, :depth]

    def dot(a, b):
        return jnp.dot(a, b, preferred_element_type=f32)

    return dot(low, table_high) + dot(high, table_low) + dot(high, table_high)


def packing(chunk, steps):
    full, tail = steps // LANES, steps % LANES
    folds = 1
    if tail:
        folds = max(f for f in range(1, LANES // tail + 1) if chunk % (8 * f) == 0 or f == 1)
    tail_rows = chunk // folds if tail else 0
    return full, tail, folds, tail_rows


def pack_into(ref, value, chunk, steps):
    full, tail, folds, tail_rows = packing(chunk, steps)
    for c in range(full):
        ref[c * chunk : (c + 1) * chunk] = value[:, c * LANES : (c + 1) * LANES]
    if tail:
        last = value[:, full * LANES :]
        folded = last[:tail_rows]
        for f in range(1, folds):
            folded = folded + pltpu.roll(last[f * tail_rows : (f + 1) * tail_rows], f * tail, 1)
        ref[full * chunk :] = folded


def unpacked(value, chunk, steps):
    full, tail, folds, tail_rows = packing(chunk, steps)
    columns = [value[c * chunk : (c + 1) * chunk] for c in range(full)]
    if tail:
        folded = value[full * chunk :]
        pieces = [folded] + [pltpu.roll(folded, LANES - f * tail, 1) for f in range(1, folds)]
        columns.append(jnp.concatenate(pieces, axis=0))
    return jnp.concatenate(columns, axis=1)


def kernel(
    sizes,
    x_ref,
    blocks_ref,
    weights_ref,
    fwd_hbm,
    inv_hbm,
    out_ref,
    raw,
    ft,
    fwd,
    inv,
    wide,
    xg,
    xs,
    ps,
    part,
    part_in,
    wexp,
    wdat,
    gs,
    gout,
    y_in,
    z_out,
    z_in,
    local_sem,
    gz_s,
    gz_own,
    gz_r,
    gy_s,
    gy_r,
    ps_s,
    ps_r,
    pg_s,
    pg_r,
    ry_s,
    ry_r,
    rz_s,
    rz_r,
):
    vecs, own_pars, steps, sens, pars, n_sensor, n_param, fast = sizes
    slow = n_sensor // fast
    freqs = steps + 1
    freq_pad = round_up(freqs, LANES)
    time_pad = round_up(steps, LANES)
    tiles = freq_pad // LANES
    group_pars = fast * own_pars
    chunk = own_pars * vecs
    group_rows = group_pars * vecs
    rows = sens * vecs
    share = rows // n_param
    unroll = 4 if group_pars % 4 == 0 else 1

    me = lax.axis_index("sensor")
    mp = lax.axis_index("param")
    mz = me // fast
    my = me % fast
    y_peer = mz * fast + (1 - my)

    def z_at(distance):
        return lax.rem(mz + distance, slow)

    def z_back(distance):
        return lax.rem(mz + slow - distance, slow)

    def p_at(distance):
        return lax.rem(mp + distance, n_param)

    def p_back(distance):
        return lax.rem(mp + n_param - distance, n_param)

    def to_sensor(target, src, dst, send, recv):
        return pltpu.make_async_remote_copy(
            src_ref=src, dst_ref=dst, send_sem=send, recv_sem=recv,
            device_id=(target, mp), device_id_type=pl.DeviceIdType.MESH,
        )

    def to_param(target, src, dst, send, recv):
        return pltpu.make_async_remote_copy(
            src_ref=src, dst_ref=dst, send_sem=send, recv_sem=recv,
            device_id=(me, target), device_id_type=pl.DeviceIdType.MESH,
        )

    barrier = pltpu.get_barrier_semaphore()

    def greet(device):
        pl.semaphore_signal(barrier, inc=1, device_id=device, device_id_type=pl.DeviceIdType.MESH)

    greet((y_peer, mp))
    for d in range(1, slow):
        greet((z_at(d) * fast + my, mp))
    for j in range(1, n_param):
        greet((me, p_at(j)))

    blocks_rows = blocks_ref.shape[0]
    load_blocks = pltpu.make_async_copy(
        blocks_ref.at[:, 0], raw.at[pl.ds(0, blocks_rows)], local_sem.at[0]
    )
    load_blocks.start()
    load_fwd = pltpu.make_async_copy(fwd_hbm, fwd, local_sem.at[1])
    load_fwd.start()
    load_inv = pltpu.make_async_copy(inv_hbm, inv, local_sem.at[2])
    load_inv.start()
    wide[...] = jnp.zeros_like(wide)
    wide[:, :steps] = x_ref[...]
    pack_into(xg.at[me], wide[...], chunk, steps)
    pl.semaphore_wait(barrier, 1 + (slow - 1) + (n_param - 1))

    def right_copy(source, send):
        ref = xg.at[source * fast + my]
        return to_sensor((mz + 1) * fast + my, ref, ref, send, gz_r.at[source])

    def left_copy(source, send):
        ref = xg.at[source * fast + my]
        return to_sensor((mz - 1) * fast + my, ref, ref, send, gz_r.at[source])

    def y_copy(source):
        ref = xg.at[source * fast + my]
        return to_sensor(y_peer, ref, ref, gy_s.at[source], gy_r.at[source])

    @pl.when(mz + 1 < slow)
    def _():
        right_copy(mz, gz_s.at[mz]).start()

    @pl.when(mz > 0)
    def _():
        left_copy(mz, gz_own.at[0]).start()

    y_copy(mz).start()

    spread = jnp.concatenate(
        [jnp.broadcast_to(weights_ref[r : r + 1], (vecs, steps)) for r in range(sens)], axis=0
    )
    for i in range(n_param):
        wexp[i] = spread[i * share : (i + 1) * share]

    def turn(part_index, tile):
        width_tiles = (pars * sens) // LANES
        first = pl.multiple_of(tile * LANES, LANES)
        inside = first + lax.broadcasted_iota(jnp.int32, (LANES, LANES), 1) < freqs
        for w in range(width_tiles):
            start = (part_index * freqs + first) * width_tiles + w
            block = raw[pl.ds(start, LANES, stride=width_tiles), :]
            turned = jnp.where(inside, block.T, 0.0)
            per = LANES // sens
            ft[part_index, w * per : (w + 1) * per, :, pl.ds(first, LANES)] = turned.reshape(
                per, sens, LANES
            )

    load_blocks.wait()

    def turn_tile(tile, carry):
        turn(0, tile)
        turn(1, tile)
        return carry

    lax.fori_loop(0, tiles, turn_tile, 0)
    load_fwd.wait()

    def lanes_of(tile, c):
        return pl.ds(pl.multiple_of(tile * LANES + c * freq_pad, LANES), LANES)

    def forward_group(zz):
        field = jnp.concatenate(
            [unpacked(xg[zz * fast + y], chunk, steps) for y in range(fast)], axis=0
        )
        xs[...] = product(field, fwd, time_pad).reshape(group_pars, vecs, 2 * freq_pad)
        base = zz * group_pars

        def tile_step(tile, carry):
            re, im = lanes_of(tile, 0), lanes_of(tile, 1)
            acc = tuple(ps[r, :, re] for r in range(sens)) + tuple(
                ps[r, :, im] for r in range(sens)
            )

            def par_step(step, acc):
                acc = list(acc)
                for u in range(unroll):
                    q = step * unroll + u
                    xr, xi = xs[q, :, re], xs[q, :, im]
                    for r in range(sens):
                        fr = ft[0, base + q, r : r + 1, re]
                        fi = ft[1, base + q, r : r + 1, re]
                        acc[r] = acc[r] + fr * xr - fi * xi
                        acc[sens + r] = acc[sens + r] + fr * xi + fi * xr
                return tuple(acc)

            acc = lax.fori_loop(0, group_pars // unroll, par_step, acc)
            for r in range(sens):
                ps[r, :, re] = acc[r]
                ps[r, :, im] = acc[sens + r]
            return carry

        lax.fori_loop(0, tiles, tile_step, 0)

    inner = jnp.minimum(mz, slow - 1 - mz)

    def place_of(n):
        near = (n + 1) // 2
        left = jnp.where(n <= 2 * inner, n % 2 == 1, mz > inner)
        distance = jnp.where(n <= 2 * inner, near, n - inner)
        return jnp.where(left, mz - distance, mz + distance)

    ps[...] = jnp.zeros_like(ps)

    def gather_step(n, carry):
        @pl.when(n + 1 < slow)
        def _():
            source = place_of(n + 1)
            right_copy(source, gz_s.at[source]).wait_recv()

            @pl.when((source < mz) & (mz + 1 < slow))
            def _():
                right_copy(source, gz_s.at[source]).start()

            @pl.when((source > mz) & (mz > 0))
            def _():
                left_copy(source, gz_s.at[source]).start()

            y_copy(source).start()

        zz = place_of(n)
        y_copy(zz).wait_recv()
        forward_group(zz)
        return carry

    lax.fori_loop(0, slow, gather_step, 0)

    load_inv.wait()
    series = product(ps[...].reshape(rows, 2 * freq_pad), inv, 2 * freq_pad)
    for i in range(n_param):
        part[i] = series[i * share : (i + 1) * share, :steps]
    sums = {}
    for j in range(1, n_param):
        sums[j] = to_param(p_at(j), part.at[p_at(j)], part_in.at[j], ps_s.at[j], ps_r.at[j])
        sums[j].start()
    total = part[mp]
    for j in range(1, n_param):
        sums[j].wait_recv()
        total = total + part_in[j]
    wdat[mp] = total * wexp[mp]
    spreads = {}
    for j in range(1, n_param):
        spreads[j] = to_param(p_at(j), wdat.at[mp], wdat.at[mp], pg_s.at[j], pg_r.at[j])
        spreads[j].start()
    for j in range(1, n_param):
        spreads[j].wait_recv()
    weighted = jnp.concatenate([wdat[i] for i in range(n_param)], axis=0)
    ps[...] = product(weighted, fwd, steps).reshape(sens, vecs, 2 * freq_pad)

    def adjoint_group(zz, slot):
        base = zz * group_pars

        def tile_step(tile, carry):
            re, im = lanes_of(tile, 0), lanes_of(tile, 1)
            wr = [ps[r, :, re] for r in range(sens)]
            wi = [ps[r, :, im] for r in range(sens)]

            def par_step(step, carry):
                for u in range(unroll):
                    q = step * unroll + u
                    gr = jnp.zeros((vecs, LANES), f32)
                    gi = jnp.zeros((vecs, LANES), f32)
                    for r in range(sens):
                        fr = ft[0, base + q, r : r + 1, re]
                        fi = ft[1, base + q, r : r + 1, re]
                        gr = gr + fr * wr[r] + fi * wi[r]
                        gi = gi + fr * wi[r] - fi * wr[r]
                    gs[q, :, re] = gr
                    gs[q, :, im] = gi
                return carry

            return lax.fori_loop(0, group_pars // unroll, par_step, carry)

        lax.fori_loop(0, tiles, tile_step, 0)
        result = product(gs[...].reshape(group_rows, 2 * freq_pad), inv, 2 * freq_pad)
        for y in range(fast):
            pack_into(gout.at[slot, y], result[y * chunk : (y + 1) * chunk], chunk, steps)

    y_sends, z_sends = {}, {}

    def pass_on(d):
        y_sends[d].wait_recv()
        z_out[d] = gout[d, my] + y_in[d]
        z_sends[d] = to_sensor(z_at(d) * fast + my, z_out.at[d], z_in.at[d], rz_s.at[d], rz_r.at[d])
        z_sends[d].start()

    order = list(range(slow - 1, -1, -1))
    for place, d in enumerate(order):
        adjoint_group(z_at(d), d)
        y_sends[d] = to_sensor(y_peer, gout.at[d, 1 - my], y_in.at[d], ry_s.at[d], ry_r.at[d])
        y_sends[d].start()
        if place:
            pass_on(order[place - 1])
    y_sends[0].wait_recv()
    answer = gout[0, my] + y_in[0]
    for d in order[:-1]:
        z_sends[d].wait_recv()
        answer = answer + z_in[d]
    out_ref[...] = unpacked(answer, chunk, steps)[:, :steps]

    @pl.when(mz > 0)
    def _():
        left_copy(mz, gz_own.at[0]).wait_send()

    def drain(source, carry):
        y_copy(source).wait_send()

        @pl.when((source <= mz) & (mz + 1 < slow))
        def _():
            right_copy(source, gz_s.at[source]).wait_send()

        @pl.when((source > mz) & (mz > 0))
        def _():
            left_copy(source, gz_s.at[source]).wait_send()

        return carry

    lax.fori_loop(0, slow, drain, 0)
    for d in range(1, slow):
        z_sends[d].wait_send()
    for d in range(slow):
        y_sends[d].wait_send()
    for j in range(1, n_param):
        sums[j].wait_send()
        spreads[j].wait_send()


def shards(n_sensor, n_param, parameter_field, operator_blocks, noise_weights):
    vecs, own_pars, steps = parameter_field.shape
    sens = noise_weights.shape[0]
    freqs = steps + 1
    flat_width = operator_blocks.shape[4]
    pars = flat_width // sens
    fast = 2
    slow = n_sensor // fast
    chunk = own_pars * vecs
    group_pars = fast * own_pars
    share = sens * vecs // n_param
    freq_pad = round_up(freqs, LANES)
    width_tiles = flat_width // LANES
    forward_table, inverse_table = tables(steps)
    field = jnp.transpose(parameter_field, (1, 0, 2)).reshape(chunk, steps)
    blocks = operator_blocks.reshape(2 * freqs * width_tiles, 1, LANES)
    sizes = (vecs, own_pars, steps, sens, pars, n_sensor, n_param, fast)
    full, _, _, tail_rows = packing(chunk, steps)
    packed_rows = full * chunk + tail_rows
    raw_rows = round_up((freqs + freq_pad) * width_tiles, 8)
    vmem = pl.BlockSpec(memory_space=pltpu.VMEM)
    anywhere = pl.BlockSpec(memory_space=pl.ANY)
    dma = pltpu.SemaphoreType.DMA
    result = pl.pallas_call(
        functools.partial(kernel, sizes),
        out_shape=jax.ShapeDtypeStruct((chunk, steps), f32),
        in_specs=[vmem, anywhere, vmem, anywhere, anywhere],
        out_specs=vmem,
        scratch_shapes=[
            pltpu.VMEM((raw_rows, LANES), f32),
            pltpu.VMEM((2, pars, sens, freq_pad), f32),
            pltpu.VMEM(forward_table.shape, bf16),
            pltpu.VMEM(inverse_table.shape, bf16),
            pltpu.VMEM((chunk, round_up(steps, LANES)), f32),
            pltpu.VMEM((n_sensor, packed_rows, LANES), f32),
            pltpu.VMEM((group_pars, vecs, 2 * freq_pad), f32),
            pltpu.VMEM((sens, vecs, 2 * freq_pad), f32),
            pltpu.VMEM((n_param, share, steps), f32),
            pltpu.VMEM((n_param, share, steps), f32),
            pltpu.VMEM((n_param, share, steps), f32),
            pltpu.VMEM((n_param, share, steps), f32),
            pltpu.VMEM((group_pars, vecs, 2 * freq_pad), f32),
            pltpu.VMEM((slow, fast, packed_rows, LANES), f32),
            pltpu.VMEM((slow, packed_rows, LANES), f32),
            pltpu.VMEM((slow, packed_rows, LANES), f32),
            pltpu.VMEM((slow, packed_rows, LANES), f32),
            dma((3,)),
            dma((slow,)),
            dma((1,)),
            dma((slow,)),
            dma((slow,)),
            dma((slow,)),
            dma((n_param,)),
            dma((n_param,)),
            dma((n_param,)),
            dma((n_param,)),
            dma((slow,)),
            dma((slow,)),
            dma((slow,)),
            dma((slow,)),
        ],
        compiler_params=pltpu.CompilerParams(
            collective_id=0, has_side_effects=True, vmem_limit_bytes=60 * 1024 * 1024
        ),
    )(field, blocks, noise_weights, jnp.asarray(forward_table), jnp.asarray(inverse_table))
    return jnp.transpose(result.reshape(own_pars, vecs, steps), (1, 0, 2))


def solution(mesh):
    in_specs = (
        P(None, ("param", "sensor"), None),
        P(None, None, "sensor", "param", None),
        P("sensor", None),
    )
    out_specs = P(None, ("param", "sensor"), None)
    run = functools.partial(shards, mesh.shape["sensor"], mesh.shape["param"])
    return jax.shard_map(run, mesh=mesh, in_specs=in_specs, out_specs=out_specs, check_vma=False)
```

```python
import functools
import math

import jax
import jax.numpy as jnp
import ml_dtypes
import numpy as np
from jax import lax
from jax.experimental import pallas as pl
from jax.experimental.pallas import tpu as pltpu
from jax.sharding import PartitionSpec as P

LANES = 128
f32 = jnp.float32
bf16 = jnp.bfloat16


def round_up(value, step):
    return -(-value // step) * step


def split_table(table):
    high = table.astype(ml_dtypes.bfloat16)
    low = (table - high.astype(np.float64)).astype(ml_dtypes.bfloat16)
    return np.stack([high, low])


def tables(time_steps):
    length = 2 * time_steps
    freq_count = time_steps + 1
    time_pad = round_up(time_steps, LANES)
    freq_pad = round_up(freq_count, LANES)
    angles = (np.arange(time_steps)[:, None] * np.arange(freq_count)[None, :] % length) * (
        2.0 * math.pi / length
    )
    factor = np.full(freq_count, 2.0)
    factor[0] = factor[-1] = 1.0
    factor /= length
    forward = np.zeros((time_pad, 2 * freq_pad))
    forward[:time_steps, :freq_count] = np.cos(angles)
    forward[:time_steps, freq_pad : freq_pad + freq_count] = -np.sin(angles)
    inverse = np.zeros((2 * freq_pad, time_pad))
    inverse[:freq_count, :time_steps] = factor[:, None] * np.cos(angles).T
    inverse[freq_pad : freq_pad + freq_count, :time_steps] = -factor[:, None] * np.sin(angles).T
    return split_table(forward), split_table(inverse)


def product(left, table_ref, depth):
    high = left.astype(bf16)
    low = (left - high.astype(f32)).astype(bf16)
    table_high = table_ref[0, :depth]
    table_low = table_ref[1, :depth]

    def dot(a, b):
        return jnp.dot(a, b, preferred_element_type=f32)

    return dot(low, table_high) + dot(high, table_low) + dot(high, table_high)


def packing(chunk, steps):
    full, tail = steps // LANES, steps % LANES
    folds = 1
    if tail:
        folds = max(f for f in range(1, LANES // tail + 1) if chunk % (8 * f) == 0 or f == 1)
    tail_rows = chunk // folds if tail else 0
    return full, tail, folds, tail_rows


def pack_into(ref, value, chunk, steps):
    full, tail, folds, tail_rows = packing(chunk, steps)
    for c in range(full):
        ref[c * chunk : (c + 1) * chunk] = value[:, c * LANES : (c + 1) * LANES]
    if tail:
        last = value[:, full * LANES :]
        folded = last[:tail_rows]
        for f in range(1, folds):
            folded = folded + pltpu.roll(last[f * tail_rows : (f + 1) * tail_rows], f * tail, 1)
        ref[full * chunk :] = folded


def unpacked(value, chunk, steps):
    full, tail, folds, tail_rows = packing(chunk, steps)
    columns = [value[c * chunk : (c + 1) * chunk] for c in range(full)]
    if tail:
        folded = value[full * chunk :]
        pieces = [folded] + [pltpu.roll(folded, LANES - f * tail, 1) for f in range(1, folds)]
        columns.append(jnp.concatenate(pieces, axis=0))
    return jnp.concatenate(columns, axis=1)


def kernel(
    sizes,
    x_ref,
    blocks_ref,
    weights_ref,
    fwd_hbm,
    inv_hbm,
    out_ref,
    raw,
    ft,
    fwd,
    inv,
    wide,
    xg,
    xs,
    ps,
    part,
    part_in,
    wexp,
    wdat,
    gs,
    gout,
    y_in,
    z_out,
    z_in,
    local_sem,
    gz_s,
    gz_own,
    gz_r,
    gy_s,
    gy_r,
    ps_s,
    ps_r,
    pg_s,
    pg_r,
    ry_s,
    ry_r,
    rz_s,
    rz_r,
):
    vecs, own_pars, steps, sens, pars, n_sensor, n_param, fast = sizes
    slow = n_sensor // fast
    freqs = steps + 1
    freq_pad = round_up(freqs, LANES)
    time_pad = round_up(steps, LANES)
    tiles = freq_pad // LANES
    group_pars = fast * own_pars
    chunk = own_pars * vecs
    group_rows = group_pars * vecs
    rows = sens * vecs
    share = rows // n_param
    packed_rows = xg.shape[1]
    pieces = 2 if packed_rows % 16 == 0 else 1
    piece_rows = packed_rows // pieces
    unroll = 4 if group_pars % 4 == 0 else 1

    me = lax.axis_index("sensor")
    mp = lax.axis_index("param")
    mz = me // fast
    my = me % fast
    y_peer = mz * fast + (1 - my)

    def z_at(distance):
        return lax.rem(mz + distance, slow)

    def z_back(distance):
        return lax.rem(mz + slow - distance, slow)

    def p_at(distance):
        return lax.rem(mp + distance, n_param)

    def p_back(distance):
        return lax.rem(mp + n_param - distance, n_param)

    def to_sensor(target, src, dst, send, recv):
        return pltpu.make_async_remote_copy(
            src_ref=src, dst_ref=dst, send_sem=send, recv_sem=recv,
            device_id=(target, mp), device_id_type=pl.DeviceIdType.MESH,
        )

    def to_param(target, src, dst, send, recv):
        return pltpu.make_async_remote_copy(
            src_ref=src, dst_ref=dst, send_sem=send, recv_sem=recv,
            device_id=(me, target), device_id_type=pl.DeviceIdType.MESH,
        )

    barrier = pltpu.get_barrier_semaphore()

    def greet(device):
        pl.semaphore_signal(barrier, inc=1, device_id=device, device_id_type=pl.DeviceIdType.MESH)

    greet((y_peer, mp))
    for d in range(1, slow):
        greet((z_at(d) * fast + my, mp))
    for j in range(1, n_param):
        greet((me, p_at(j)))

    blocks_rows = blocks_ref.shape[0]
    load_blocks = pltpu.make_async_copy(
        blocks_ref.at[:, 0], raw.at[pl.ds(0, blocks_rows)], local_sem.at[0]
    )
    load_blocks.start()
    load_fwd = pltpu.make_async_copy(fwd_hbm, fwd, local_sem.at[1])
    load_fwd.start()
    load_inv = pltpu.make_async_copy(inv_hbm, inv, local_sem.at[2])
    load_inv.start()
    wide[...] = jnp.zeros_like(wide)
    wide[:, :steps] = x_ref[...]
    pack_into(xg.at[me], wide[...], chunk, steps)
    pl.semaphore_wait(barrier, 1 + (slow - 1) + (n_param - 1))

    def piece(h):
        return pl.ds(h * piece_rows, piece_rows)

    def right_copy(source, h):
        ref = xg.at[source * fast + my, piece(h)]
        slot = source * pieces + h
        return to_sensor((mz + 1) * fast + my, ref, ref, gz_s.at[slot], gz_r.at[slot])

    def left_copy(source, h, own=False):
        ref = xg.at[source * fast + my, piece(h)]
        slot = source * pieces + h
        send = gz_own.at[h] if own else gz_s.at[slot]
        return to_sensor((mz - 1) * fast + my, ref, ref, send, gz_r.at[slot])

    def y_copy(source, h):
        ref = xg.at[source * fast + my, piece(h)]
        slot = source * pieces + h
        return to_sensor(y_peer, ref, ref, gy_s.at[slot], gy_r.at[slot])

    for h in range(pieces):

        @pl.when(mz + 1 < slow)
        def _():
            right_copy(mz, h).start()

        @pl.when(mz > 0)
        def _():
            left_copy(mz, h, True).start()

        y_copy(mz, h).start()

    spread = jnp.concatenate(
        [jnp.broadcast_to(weights_ref[r : r + 1], (vecs, steps)) for r in range(sens)], axis=0
    )
    for i in range(n_param):
        wexp[i] = spread[i * share : (i + 1) * share]

    def turn(part_index, tile):
        width_tiles = (pars * sens) // LANES
        first = pl.multiple_of(tile * LANES, LANES)
        inside = first + lax.broadcasted_iota(jnp.int32, (LANES, LANES), 1) < freqs
        for w in range(width_tiles):
            start = (part_index * freqs + first) * width_tiles + w
            block = raw[pl.ds(start, LANES, stride=width_tiles), :]
            turned = jnp.where(inside, block.T, 0.0)
            per = LANES // sens
            ft[part_index, w * per : (w + 1) * per, :, pl.ds(first, LANES)] = turned.reshape(
                per, sens, LANES
            )

    load_blocks.wait()

    def turn_tile(tile, carry):
        turn(0, tile)
        turn(1, tile)
        return carry

    lax.fori_loop(0, tiles, turn_tile, 0)
    load_fwd.wait()

    def lanes_of(tile, c):
        return pl.ds(pl.multiple_of(tile * LANES + c * freq_pad, LANES), LANES)

    def forward_group(zz):
        field = jnp.concatenate(
            [unpacked(xg[zz * fast + y], chunk, steps) for y in range(fast)], axis=0
        )
        xs[...] = product(field, fwd, time_pad).reshape(group_pars, vecs, 2 * freq_pad)
        base = zz * group_pars

        def tile_step(tile, carry):
            re, im = lanes_of(tile, 0), lanes_of(tile, 1)
            acc = tuple(ps[r, :, re] for r in range(sens)) + tuple(
                ps[r, :, im] for r in range(sens)
            )

            def par_step(step, acc):
                acc = list(acc)
                for u in range(unroll):
                    q = step * unroll + u
                    xr, xi = xs[q, :, re], xs[q, :, im]
                    for r in range(sens):
                        fr = ft[0, base + q, r : r + 1, re]
                        fi = ft[1, base + q, r : r + 1, re]
                        acc[r] = acc[r] + fr * xr - fi * xi
                        acc[sens + r] = acc[sens + r] + fr * xi + fi * xr
                return tuple(acc)

            acc = lax.fori_loop(0, group_pars // unroll, par_step, acc)
            for r in range(sens):
                ps[r, :, re] = acc[r]
                ps[r, :, im] = acc[sens + r]
            return carry

        lax.fori_loop(0, tiles, tile_step, 0)

    inner = jnp.minimum(mz, slow - 1 - mz)

    def place_of(n):
        near = (n + 1) // 2
        left = jnp.where(n <= 2 * inner, n % 2 == 1, mz > inner)
        distance = jnp.where(n <= 2 * inner, near, n - inner)
        return jnp.where(left, mz - distance, mz + distance)

    ps[...] = jnp.zeros_like(ps)

    def gather_step(n, carry):
        @pl.when(n + 1 < slow)
        def _():
            source = place_of(n + 1)
            for h in range(pieces):
                right_copy(source, h).wait_recv()

                @pl.when((source < mz) & (mz + 1 < slow))
                def _():
                    right_copy(source, h).start()

                @pl.when((source > mz) & (mz > 0))
                def _():
                    left_copy(source, h).start()

                y_copy(source, h).start()

        zz = place_of(n)
        for h in range(pieces):
            y_copy(zz, h).wait_recv()
        forward_group(zz)
        return carry

    lax.fori_loop(0, slow, gather_step, 0)

    load_inv.wait()
    series = product(ps[...].reshape(rows, 2 * freq_pad), inv, 2 * freq_pad)
    for i in range(n_param):
        part[i] = series[i * share : (i + 1) * share, :steps]
    sums = {}
    for j in range(1, n_param):
        sums[j] = to_param(p_at(j), part.at[p_at(j)], part_in.at[j], ps_s.at[j], ps_r.at[j])
        sums[j].start()
    total = part[mp]
    for j in range(1, n_param):
        sums[j].wait_recv()
        total = total + part_in[j]
    wdat[mp] = total * wexp[mp]
    spreads = {}
    for j in range(1, n_param):
        spreads[j] = to_param(p_at(j), wdat.at[mp], wdat.at[mp], pg_s.at[j], pg_r.at[j])
        spreads[j].start()
    for j in range(1, n_param):
        spreads[j].wait_recv()
    weighted = jnp.concatenate([wdat[i] for i in range(n_param)], axis=0)
    ps[...] = product(weighted, fwd, steps).reshape(sens, vecs, 2 * freq_pad)

    def adjoint_group(zz, slot):
        base = zz * group_pars

        def tile_step(tile, carry):
            re, im = lanes_of(tile, 0), lanes_of(tile, 1)
            wr = [ps[r, :, re] for r in range(sens)]
            wi = [ps[r, :, im] for r in range(sens)]

            def par_step(step, carry):
                for u in range(unroll):
                    q = step * unroll + u
                    gr = jnp.zeros((vecs, LANES), f32)
                    gi = jnp.zeros((vecs, LANES), f32)
                    for r in range(sens):
                        fr = ft[0, base + q, r : r + 1, re]
                        fi = ft[1, base + q, r : r + 1, re]
                        gr = gr + fr * wr[r] + fi * wi[r]
                        gi = gi + fr * wi[r] - fi * wr[r]
                    gs[q, :, re] = gr
                    gs[q, :, im] = gi
                return carry

            return lax.fori_loop(0, group_pars // unroll, par_step, carry)

        lax.fori_loop(0, tiles, tile_step, 0)
        result = product(gs[...].reshape(group_rows, 2 * freq_pad), inv, 2 * freq_pad)
        for y in range(fast):
            pack_into(gout.at[slot, y], result[y * chunk : (y + 1) * chunk], chunk, steps)

    y_sends, z_sends = {}, {}

    def pass_on(d):
        for h in range(pieces):
            y_sends[d, h].wait_recv()
            z_out[d, piece(h)] = gout[d, my, piece(h)] + y_in[d, piece(h)]
            slot = d * pieces + h
            z_sends[d, h] = to_sensor(
                z_at(d) * fast + my, z_out.at[d, piece(h)], z_in.at[d, piece(h)],
                rz_s.at[slot], rz_r.at[slot],
            )
            z_sends[d, h].start()

    order = list(range(slow - 1, -1, -1))
    for place, d in enumerate(order):
        adjoint_group(z_at(d), d)
        for h in range(pieces):
            slot = d * pieces + h
            y_sends[d, h] = to_sensor(
                y_peer, gout.at[d, 1 - my, piece(h)], y_in.at[d, piece(h)],
                ry_s.at[slot], ry_r.at[slot],
            )
            y_sends[d, h].start()
        if place >= 2:
            pass_on(order[place - 2])
    if slow > 1:
        pass_on(1)
    for h in range(pieces):
        y_sends[0, h].wait_recv()
    answer = gout[0, my] + y_in[0]
    for d in order[:-1]:
        for h in range(pieces):
            z_sends[d, h].wait_recv()
        answer = answer + z_in[d]
    out_ref[...] = unpacked(answer, chunk, steps)[:, :steps]

    for h in range(pieces):

        @pl.when(mz > 0)
        def _():
            left_copy(mz, h, True).wait_send()

    def drain(source, carry):
        for h in range(pieces):
            y_copy(source, h).wait_send()

            @pl.when((source <= mz) & (mz + 1 < slow))
            def _():
                right_copy(source, h).wait_send()

            @pl.when((source > mz) & (mz > 0))
            def _():
                left_copy(source, h).wait_send()

        return carry

    lax.fori_loop(0, slow, drain, 0)
    for copy in list(z_sends.values()) + list(y_sends.values()):
        copy.wait_send()
    for j in range(1, n_param):
        sums[j].wait_send()
        spreads[j].wait_send()


def shards(n_sensor, n_param, parameter_field, operator_blocks, noise_weights):
    vecs, own_pars, steps = parameter_field.shape
    sens = noise_weights.shape[0]
    freqs = steps + 1
    flat_width = operator_blocks.shape[4]
    pars = flat_width // sens
    fast = 2
    slow = n_sensor // fast
    chunk = own_pars * vecs
    group_pars = fast * own_pars
    share = sens * vecs // n_param
    freq_pad = round_up(freqs, LANES)
    width_tiles = flat_width // LANES
    forward_table, inverse_table = tables(steps)
    field = jnp.transpose(parameter_field, (1, 0, 2)).reshape(chunk, steps)
    blocks = operator_blocks.reshape(2 * freqs * width_tiles, 1, LANES)
    sizes = (vecs, own_pars, steps, sens, pars, n_sensor, n_param, fast)
    full, _, _, tail_rows = packing(chunk, steps)
    packed_rows = full * chunk + tail_rows
    raw_rows = round_up((freqs + freq_pad) * width_tiles, 8)
    vmem = pl.BlockSpec(memory_space=pltpu.VMEM)
    anywhere = pl.BlockSpec(memory_space=pl.ANY)
    dma = pltpu.SemaphoreType.DMA
    result = pl.pallas_call(
        functools.partial(kernel, sizes),
        out_shape=jax.ShapeDtypeStruct((chunk, steps), f32),
        in_specs=[vmem, anywhere, vmem, anywhere, anywhere],
        out_specs=vmem,
        scratch_shapes=[
            pltpu.VMEM((raw_rows, LANES), f32),
            pltpu.VMEM((2, pars, sens, freq_pad), f32),
            pltpu.VMEM(forward_table.shape, bf16),
            pltpu.VMEM(inverse_table.shape, bf16),
            pltpu.VMEM((chunk, round_up(steps, LANES)), f32),
            pltpu.VMEM((n_sensor, packed_rows, LANES), f32),
            pltpu.VMEM((group_pars, vecs, 2 * freq_pad), f32),
            pltpu.VMEM((sens, vecs, 2 * freq_pad), f32),
            pltpu.VMEM((n_param, share, steps), f32),
            pltpu.VMEM((n_param, share, steps), f32),
            pltpu.VMEM((n_param, share, steps), f32),
            pltpu.VMEM((n_param, share, steps), f32),
            pltpu.VMEM((group_pars, vecs, 2 * freq_pad), f32),
            pltpu.VMEM((slow, fast, packed_rows, LANES), f32),
            pltpu.VMEM((slow, packed_rows, LANES), f32),
            pltpu.VMEM((slow, packed_rows, LANES), f32),
            pltpu.VMEM((slow, packed_rows, LANES), f32),
            dma((3,)),
            dma((2 * slow,)),
            dma((2,)),
            dma((2 * slow,)),
            dma((2 * slow,)),
            dma((2 * slow,)),
            dma((n_param,)),
            dma((n_param,)),
            dma((n_param,)),
            dma((n_param,)),
            dma((2 * slow,)),
            dma((2 * slow,)),
            dma((2 * slow,)),
            dma((2 * slow,)),
        ],
        compiler_params=pltpu.CompilerParams(
            collective_id=0, has_side_effects=True, vmem_limit_bytes=60 * 1024 * 1024
        ),
    )(field, blocks, noise_weights, jnp.asarray(forward_table), jnp.asarray(inverse_table))
    return jnp.transpose(result.reshape(own_pars, vecs, steps), (1, 0, 2))


def solution(mesh):
    in_specs = (
        P(None, ("param", "sensor"), None),
        P(None, None, "sensor", "param", None),
        P("sensor", None),
    )
    out_specs = P(None, ("param", "sensor"), None)
    run = functools.partial(shards, mesh.shape["sensor"], mesh.shape["param"])
    return jax.shard_map(run, mesh=mesh, in_specs=in_specs, out_specs=out_specs, check_vma=False)
```
